32 devices in a mesh: groups: 2 (over y), train: 8 (over z, x), query: 2 (over core).
Axes of the slice: x: 2, y: 2, z: 4, core: 2. Of those that a mesh axis runs over, the one named last changes fastest.
Arguments:
- train_grads: bfloat16 [12288, 4096], P(('groups', 'train'), 'query'), parts along dimension 0, may hold values from -6 to 6
- query_grads: bfloat16 [512, 4096], P(('groups', 'train'), 'query'), parts along dimension 0, may hold values from -6 to 6
- precond: bfloat16 [8, 512, 512], P('query'), may hold values from -0.25 to 0.25
- pairs: int32 [96, 2], P(('groups', 'train')), parts along dimension 0, may hold values from 0 to 7, all different within a row; in each aligned block of 6 rows (0 to 5, 6 to 11, ...) at most 3 rows name the same one
Outputs:
- top_scores: float32 [512, 16], P(('groups', 'train', 'query')), parts along dimension 0
The draws below stay inside these ranges and needn't reach their ends.
There are 2 independent parts, one for each index of `groups`. The reference program is written for one: setup_inputs(seed, part) draws one part's arguments, and reference() takes and returns one part's arrays. A program takes and returns all parts, laid end to end along the dimension named above; an argument that names none is the same for every part. Nothing has to cross between parts.
Inputs may be any that keep to these rules, and one draw needn't show every extreme that they name: `pairs`: each row names 2 different query blocks. Within each aligned block of 6 rows (the training blocks of one index of train) no query block is named more than 3 times, and some query block exactly 3 times. Every query block is named by some row.
All inputs are finite; a program needn't handle non-finite values.
Results may differ from the reference program's by a relative error of at most 0.0014.
Values may be sent and summed in bfloat16 or wider, within the bound.
A program may use at most 64 MiB of HBM per device.

```python
import math
import jax
import jax.numpy as jnp
import numpy as np
from jax import lax

K = 4096
KB = 512
TBLK = 128
TOPM = 16
TB_DEV = 6
Q_DEV = 32
NTB = 48
NTR = 6144
QBLOCKS = 8
NQ = 256
FAN = 2
MOST = 3


def steps_of(own_key, shape, pieces, least, high):
    level, own = 1.0, jax.random.fold_in(own_key, 6)
    for position, parts in pieces:
        steps = jnp.exp(jax.random.uniform(jax.random.fold_in(own, position), (parts,), jnp.float32, least / len(pieces), high / len(pieces)))
        level = level * jnp.repeat(steps, shape[position] // parts).reshape([-1 if axis == position else 1 for axis in range(len(shape))])
    return level


def shared_out(key, own, number, rows, number_of, top, reach, lean):
    sequence = jax.random.permutation(key, number_of)
    heavy_load, ordinary = load_shares(number_of, rows * top, reach, lean, True), load_shares(number_of, rows * top, reach, lean, False)
    places = jnp.arange(number_of)

    def named(sizes, offset_by):
        used = int((sizes > 0).sum())
        fixed = max(1, used // 4)
        shifted = fixed + (places - fixed + offset_by * (used - fixed)) % max(1, number_of - fixed)
        return jnp.zeros((number_of,), jnp.int32).at[sequence[jnp.where(places < fixed, places, shifted)]].set(jnp.asarray(sizes, jnp.int32))

    sizes = jnp.where(number % 4 == 0, named(heavy_load, number // 4), named(ordinary, number - number // 4 - 1))
    mixed = jax.random.permutation(jax.random.fold_in(own, 3), number_of)
    donor, taker = mixed[0:number_of // 2 * 2:2], mixed[1:number_of // 2 * 2:2]
    room = jnp.minimum(sizes[donor] - 1, reach - sizes[taker]) // 2
    room = jnp.where((donor == sequence[0]) | (taker == sequence[0]) | (sizes[taker] == 0), 0, jnp.maximum(room, 0))
    shifted = jax.random.randint(jax.random.fold_in(own, 4), (number_of // 2,), 0, 1 << 20) % (room + 1)
    sizes = sizes.at[donor].add(-shifted).at[taker].add(shifted)
    labels = jnp.searchsorted(jnp.cumsum(sizes), jnp.arange(rows * top), side="right").astype(jnp.int32)
    grid = labels.reshape(top, rows).T
    grid = grid[jax.random.permutation(jax.random.fold_in(own, 1), rows)]
    offset_by = jax.random.randint(jax.random.fold_in(own, 2), (rows, 1), 0, top)
    return jnp.take_along_axis(grid, (jnp.arange(top)[None, :] + offset_by) % top, axis=1)


def load_shares(number_of, total, reach, slope, full):
    portions = [(1 << 20) // math.isqrt(standing ** slope) + 1 for standing in range(1, number_of + 1)]
    largest = reach if full else min(reach, max(-(-total // number_of), total * portions[0] // sum(portions)))
    least = 1 if total - largest >= number_of - 1 else 0
    counts, rest = [largest] + [least] * (number_of - 1), total - largest - least * (number_of - 1)
    while rest > 0:
        candidates = [i for i in range(1, number_of) if counts[i] < largest] or [i for i in range(1, number_of) if counts[i] < reach]
        pool, left = sum([portions[i] for i in candidates]), rest
        for i in candidates:
            more = min(reach - counts[i], max(1, left * portions[i] // pool), rest)
            counts[i] = counts[i] + more
            rest = rest - more
    return np.array(counts)


def scatter_about(rng, dims, width, limit, split=(), dtype=jnp.bfloat16):
    values = jax.random.normal(rng, dims, jnp.float32) * width
    if len(split) > 0:
        values = steps_of(rng, dims, split, -0.22, 0.18) * values
    return jnp.clip(values, min=-limit, max=limit).astype(dtype)


def setup_inputs(seed: int = 0, part: int = 0) -> dict:
    arg_keys = jax.random.split(jax.random.key(seed), 5)
    part_splits = jax.random.split(jax.random.fold_in(arg_keys[4], part), 5)
    train_grads = scatter_about(part_splits[0], (NTR, K), 1.0, 6.0, ((0, 8), (1, 2)))
    query_grads = scatter_about(part_splits[1], (NQ, K), 1.0, 6.0, ((0, 8), (1, 2)))
    precond = scatter_about(arg_keys[2], (K // KB, KB, KB), KB ** -0.5, 0.25, ((0, 2),))
    pairs_keys = jax.random.split(jax.random.fold_in(part_splits[3], 1), NTB // TB_DEV)
    pairs_turns = jax.random.permutation(jax.random.fold_in(part_splits[3], 3), NTB // TB_DEV)
    pairs = jax.vmap(lambda own, number: shared_out(jax.random.fold_in(part_splits[3], 2), own, number, TB_DEV, QBLOCKS, FAN, MOST, 2))(pairs_keys, pairs_turns).reshape((NTB, FAN))
    return dict(train_grads=train_grads, query_grads=query_grads, precond=precond, pairs=pairs)


empty_fill = -1e+30

def reference(train_grads, query_grads, precond, pairs):
    width_blocks = K // KB
    shaped = query_grads.reshape(NQ, width_blocks, KB).astype(jnp.float32)
    conditioned = jnp.einsum('qbk,bkj->qbj', shaped, precond.astype(jnp.float32))
    conditioned = conditioned.astype(jnp.bfloat16).reshape(QBLOCKS, Q_DEV, K)
    factor = 1.0 / math.sqrt(K)
    block_grads = train_grads.reshape(NTB, TBLK, K)

    def visit(best, inputs):
        rows_block, named_blocks = inputs
        chosen = conditioned[named_blocks].reshape(FAN * Q_DEV, K)
        tile_scores = jnp.dot(chosen, rows_block.T, preferred_element_type=jnp.float32) * factor
        tile_scores = tile_scores.reshape(FAN, Q_DEV, TBLK)
        merged = jnp.concatenate([best[named_blocks], tile_scores], axis=2)
        return (best.at[named_blocks].set(lax.top_k(merged, TOPM)[0]), None)
    initial = jnp.full((QBLOCKS, Q_DEV, TOPM), empty_fill, jnp.float32)
    best, unused = lax.scan(visit, initial, (block_grads, pairs))
    return best.reshape(NQ, TOPM)
```

```python
import functools
import math

import jax
import jax.numpy as jnp
from jax import lax
from jax.experimental import pallas as pl
from jax.experimental.pallas import tpu as pltpu
from jax.sharding import PartitionSpec as P

K = 4096
TBLK = 128
TOPM = 16
LANES = 128
MESH = pl.DeviceIdType.MESH

empty_fill = -1e30


def exchange(xs, i, j):
    a, b = xs[i], xs[j]
    xs[i], xs[j] = jnp.maximum(a, b), jnp.minimum(a, b)


def sort_falling(xs):
    xs = list(xs)
    n = len(xs)
    p = 1
    while p < n:
        k = p
        while k >= 1:
            for j in range(k % p, n - k, 2 * k):
                for i in range(min(k, n - j - k)):
                    if (i + j) // (2 * p) == (i + j + k) // (2 * p):
                        exchange(xs, i + j, i + j + k)
            k //= 2
        p *= 2
    return xs


def merge_top(xs, ys):
    n = len(xs)
    out = [jnp.maximum(xs[i], ys[n - 1 - i]) for i in range(n)]
    step = n // 2
    while step >= 1:
        for i in range(n):
            if i & step == 0:
                exchange(out, i, i + step)
        step //= 2
    return out


def merge_sublanes(xs):
    for shift in (4, 2, 1):
        xs = merge_top(xs, [pltpu.roll(x, shift, 0) for x in xs])
    return xs


def kernel(
    owners, columns, chunks,
    query_hbm, precond_hbm, train_hbm, pairs_ref, out_ref,
    query_v, precond_v, train_v, gathered, outgoing, incoming, scores, tops, arrived, flipped,
    load_sem, send_sem, recv_sem, pair_send, pair_recv, top_send, top_recv,
):
    me = lax.axis_index("train")
    core = lax.axis_index("query")
    x, z = lax.rem(me, columns), me // columns
    levels = owners // columns
    width = query_v.shape[1]
    chunk = width // chunks
    size = precond_v.shape[1]
    half = query_v.shape[0] // 2
    train_blocks = train_v.shape[0] // TBLK
    groups = owners * half // LANES
    per_group = LANES // half

    loads = [
        pltpu.make_async_copy(query_hbm, query_v, load_sem.at[0]),
        pltpu.make_async_copy(precond_hbm, precond_v, load_sem.at[1]),
        pltpu.make_async_copy(train_hbm, train_v, load_sem.at[2]),
    ]
    for load in loads:
        load.start()

    barrier = pltpu.get_barrier_semaphore()

    def greet(step, carry):
        pl.semaphore_signal(
            barrier, inc=1, device_id={"train": lax.rem(me + step, owners)}, device_id_type=MESH
        )
        return carry

    lax.fori_loop(1, owners, greet, 0)
    pl.semaphore_signal(barrier, inc=1, device_id={"query": 1 - core}, device_id_type=MESH)

    loads[0].wait()
    loads[1].wait()
    for j in range(precond_v.shape[0]):
        part = jnp.dot(
            query_v[:, j * size:(j + 1) * size], precond_v[j], preferred_element_type=jnp.float32
        ).astype(jnp.bfloat16)
        gathered[0, me, :, j * size:(j + 1) * size] = part[:half]
        gathered[1, me, :, j * size:(j + 1) * size] = part[half:]
    pl.semaphore_wait(barrier, owners)

    def piece(owner, k, way, peer):
        ref = gathered.at[:, owner, :, pl.ds(k * chunk, chunk)]
        return pltpu.make_async_remote_copy(
            src_ref=ref, dst_ref=ref,
            send_sem=send_sem.at[way, owner, k], recv_sem=recv_sem.at[owner, k],
            device_id={"train": peer}, device_id_type=MESH,
        )

    def across(owner, k, act):
        for j in range(1, columns):
            act(piece(owner, k, 1 + j, z * columns + lax.rem(x + j, columns)))

    def upward(owner, k, act):
        @pl.when(z < levels - 1)
        def _():
            act(piece(owner, k, 0, me + columns))

    def downward(owner, k, act):
        @pl.when(z > 0)
        def _():
            act(piece(owner, k, 1, me - columns))

    start = lambda copy: copy.start()
    sent = lambda copy: copy.wait_send()
    landed = lambda copy: copy.wait_recv()

    for k in range(chunks):
        upward(me, k, start)
        downward(me, k, start)
        across(me, k, start)

    def relay(hop, carry):
        for k in range(chunks):
            @pl.when(z - hop >= 0)
            def _():
                owner = me - hop * columns
                landed(piece(owner, k, 0, me))
                upward(owner, k, start)
                across(owner, k, start)

            @pl.when(z + hop < levels)
            def _():
                owner = me + hop * columns
                landed(piece(owner, k, 1, me))
                downward(owner, k, start)
                across(owner, k, start)
        return carry

    lax.fori_loop(1, levels, relay, 0)

    def collect(level, carry):
        for j in range(1, columns):
            for k in range(chunks):
                landed(piece(level * columns + lax.rem(x + j, columns), k, 1 + j, me))
        return carry

    lax.fori_loop(0, levels, collect, 0)
    loads[2].wait()

    def trade(g):
        return pltpu.make_async_remote_copy(
            src_ref=outgoing.at[g], dst_ref=incoming.at[g],
            send_sem=pair_send.at[g], recv_sem=pair_recv.at[g],
            device_id={"query": 1 - core}, device_id_type=MESH,
        )

    def product(which, g):
        rows = gathered[which, pl.ds(g * per_group, per_group)].reshape(LANES, width)
        return lax.dot_general(
            train_v[...], rows, (((1,), (1,)), ((), ())), preferred_element_type=jnp.float32
        )

    def first(g, carry):
        outgoing[g] = product(1 - core, g)
        trade(g).start()
        return carry

    lax.fori_loop(0, groups, first, 0)

    def best_of(g, carry):
        scores[...] = product(core, g)
        trade(g).wait()
        lane_owner = g * per_group + lax.broadcasted_iota(jnp.int32, (8, LANES), 1) // half

        def visit(b, best):
            named = lane_owner == pairs_ref[b, 0]
            for f in range(1, pairs_ref.shape[1]):
                named = named | (lane_owner == pairs_ref[b, f])
            vals = []
            for i in range(TBLK // 8):
                at = pl.ds(pl.multiple_of(b * TBLK + i * 8, 8), 8)
                total = scores[at, :] + incoming[g, at, :]
                vals.append(jnp.where(named, total, empty_fill))
            return tuple(merge_top(list(best), sort_falling(vals)))

        none = tuple(jnp.full((8, LANES), empty_fill, jnp.float32) for _ in range(TOPM))
        best = merge_sublanes(list(lax.fori_loop(0, train_blocks, visit, none)))
        tops[g] = jnp.concatenate([v[:1] for v in best], axis=0)
        return carry

    lax.fori_loop(0, groups, best_of, 0)

    def deliver(step):
        peer = lax.rem(me + step, owners)
        return pltpu.make_async_remote_copy(
            src_ref=tops.at[peer // per_group], dst_ref=arrived.at[me],
            send_sem=top_send.at[peer], recv_sem=top_recv.at[me],
            device_id={"train": peer}, device_id_type=MESH,
        )

    def receive(step):
        peer = lax.rem(me + step, owners)
        return pltpu.make_async_remote_copy(
            src_ref=tops.at[0], dst_ref=arrived.at[peer],
            send_sem=top_send.at[peer], recv_sem=top_recv.at[peer],
            device_id={"train": peer}, device_id_type=MESH,
        )

    def each(act):
        def body(step, carry):
            act(step)
            return carry
        lax.fori_loop(1, owners, body, 0)

    each(lambda step: deliver(step).start())
    arrived[me] = tops[me // per_group]
    for k in range(chunks):
        upward(me, k, sent)
        downward(me, k, sent)
        across(me, k, sent)

    def drain(hop, carry):
        for k in range(chunks):
            @pl.when(z - hop >= 0)
            def _():
                upward(me - hop * columns, k, sent)
                across(me - hop * columns, k, sent)

            @pl.when(z + hop < levels)
            def _():
                downward(me + hop * columns, k, sent)
                across(me + hop * columns, k, sent)
        return carry

    lax.fori_loop(1, levels, drain, 0)
    each(lambda step: receive(step).wait_recv())

    best = None
    for s in range(owners // 8):
        lists = [arrived[s * 8:(s + 1) * 8, r, :] for r in range(TOPM)]
        best = lists if best is None else merge_top(best, lists)
    best = merge_sublanes(best)
    ranked = jnp.concatenate([v[:1] for v in best], axis=0) * (1.0 / math.sqrt(K))
    square = jnp.concatenate(
        [ranked, jnp.zeros((LANES - TOPM, LANES), jnp.float32)], axis=0
    )
    flipped[...] = square.T
    mine = pl.multiple_of(lax.rem(me, per_group) * half, half)
    out_ref[...] = flipped[pl.ds(mine, half), :TOPM]
    each(lambda step: deliver(step).wait_send())


def per_device(train_grads, query_grads, precond, pairs):
    owners = lax.axis_size("train")
    columns = 1
    for c in range(2, owners):
        if owners % c == 0 and c ** 3 <= owners:
            columns = c
    queries, width = query_grads.shape
    rows = train_grads.shape[0]
    chunks = 4 if owners <= 8 else 1
    half = queries // 2
    groups = owners * half // LANES
    f32 = jnp.float32
    return pl.pallas_call(
        functools.partial(kernel, owners, columns, chunks),
        out_shape=jax.ShapeDtypeStruct((half, TOPM), f32),
        in_specs=[pl.BlockSpec(memory_space=pl.ANY)] * 3
        + [pl.BlockSpec(memory_space=pltpu.SMEM)],
        out_specs=pl.BlockSpec(memory_space=pltpu.VMEM),
        scratch_shapes=[
            pltpu.VMEM(query_grads.shape, query_grads.dtype),
            pltpu.VMEM(precond.shape, precond.dtype),
            pltpu.VMEM(train_grads.shape, train_grads.dtype),
            pltpu.VMEM((2, owners, half, width), jnp.bfloat16),
            pltpu.VMEM((groups, rows, LANES), f32),
            pltpu.VMEM((groups, rows, LANES), f32),
            pltpu.VMEM((rows, LANES), f32),
            pltpu.VMEM((groups, TOPM, LANES), f32),
            pltpu.VMEM((owners, TOPM, LANES), f32),
            pltpu.VMEM((LANES, LANES), f32),
            pltpu.SemaphoreType.DMA((3,)),
            pltpu.SemaphoreType.DMA((1 + columns, owners, chunks)),
            pltpu.SemaphoreType.DMA((owners, chunks)),
            pltpu.SemaphoreType.DMA((groups,)),
            pltpu.SemaphoreType.DMA((groups,)),
            pltpu.SemaphoreType.DMA((owners,)),
            pltpu.SemaphoreType.DMA((owners,)),
        ],
        compiler_params=pltpu.CompilerParams(
            collective_id=0, has_side_effects=True, vmem_limit_bytes=48 * 1024 * 1024
        ),
    )(query_grads, precond, train_grads, pairs)


def solution(mesh):
    placed = (
        P(("groups", "train"), "query"),
        P(("groups", "train"), "query"),
        P("query", None, None),
        P(("groups", "train"), None),
    )
    return jax.shard_map(
        per_device,
        mesh=mesh,
        in_specs=placed,
        out_specs=P(("groups", "train", "query"), None),
        check_vma=False,
    )
```

```python
import functools
import math

import jax
import jax.numpy as jnp
from jax import lax
from jax.experimental import pallas as pl
from jax.experimental.pallas import tpu as pltpu
from jax.sharding import PartitionSpec as P

K = 4096
TBLK = 128
TOPM = 16
LANES = 128
MESH = pl.DeviceIdType.MESH

empty_fill = -1e30


def exchange(xs, i, j):
    a, b = xs[i], xs[j]
    xs[i], xs[j] = jnp.maximum(a, b), jnp.minimum(a, b)


def sort_falling(xs):
    xs = list(xs)
    n = len(xs)
    p = 1
    while p < n:
        k = p
        while k >= 1:
            for j in range(k % p, n - k, 2 * k):
                for i in range(min(k, n - j - k)):
                    if (i + j) // (2 * p) == (i + j + k) // (2 * p):
                        exchange(xs, i + j, i + j + k)
            k //= 2
        p *= 2
    return xs


def merge_top(xs, ys):
    n = len(xs)
    out = [jnp.maximum(xs[i], ys[n - 1 - i]) for i in range(n)]
    step = n // 2
    while step >= 1:
        for i in range(n):
            if i & step == 0:
                exchange(out, i, i + step)
        step //= 2
    return out


def merge_sublanes(xs):
    for shift in (4, 2, 1):
        xs = merge_top(xs, [pltpu.roll(x, shift, 0) for x in xs])
    return xs


def kernel(
    owners, columns, chunks,
    query_hbm, precond_hbm, train_hbm, pairs_hbm, out_ref,
    pairs_ref, query_v, precond_v, train_v, gathered, outgoing, incoming, scores, tops, arrived,
    load_sem, send_sem, recv_sem, pair_send, pair_recv, top_send, top_recv,
):
    me = lax.axis_index("train")
    core = lax.axis_index("query")
    x, z = lax.rem(me, columns), me // columns
    levels = owners // columns
    width = query_v.shape[1]
    chunk = width // chunks
    size = precond_v.shape[1]
    half = query_v.shape[0] // 2
    train_blocks = train_v.shape[0] // TBLK
    groups = owners * half // LANES
    per_group = LANES // half

    loads = [
        pltpu.make_async_copy(query_hbm, query_v, load_sem.at[0]),
        pltpu.make_async_copy(precond_hbm, precond_v, load_sem.at[1]),
        pltpu.make_async_copy(train_hbm, train_v, load_sem.at[2]),
        pltpu.make_async_copy(pairs_hbm, pairs_ref, load_sem.at[3]),
    ]
    for load in loads:
        load.start()

    barrier = pltpu.get_barrier_semaphore()

    def greet(peer):
        pl.semaphore_signal(barrier, inc=1, device_id={"train": peer}, device_id_type=MESH)

    pl.when(z > 0)(lambda: greet(me - columns))
    pl.when(z < levels - 1)(lambda: greet(me + columns))
    for j in range(1, columns):
        greet(z * columns + lax.rem(x + j, columns))
    pl.semaphore_signal(barrier, inc=1, device_id={"query": 1 - core}, device_id_type=MESH)

    loads[0].wait()
    loads[1].wait()
    for j in range(precond_v.shape[0]):
        part = jnp.dot(
            query_v[:, j * size:(j + 1) * size], precond_v[j], preferred_element_type=jnp.float32
        ).astype(jnp.bfloat16)
        gathered[0, me, :, j * size:(j + 1) * size] = part[:half]
        gathered[1, me, :, j * size:(j + 1) * size] = part[half:]
    below, above = (z + levels - 1) // levels, (2 * levels - 2 - z) // levels
    pl.semaphore_wait(barrier, columns + below + above)

    def piece(owner, k, way, peer):
        ref = gathered.at[:, owner, :, pl.ds(k * chunk, chunk)]
        return pltpu.make_async_remote_copy(
            src_ref=ref, dst_ref=ref,
            send_sem=send_sem.at[way, owner, k], recv_sem=recv_sem.at[owner, k],
            device_id={"train": peer}, device_id_type=MESH,
        )

    def across(owner, k, act):
        for j in range(1, columns):
            act(piece(owner, k, 1 + j, z * columns + lax.rem(x + j, columns)))

    def upward(owner, k, act):
        @pl.when(z < levels - 1)
        def _():
            act(piece(owner, k, 0, me + columns))

    def downward(owner, k, act):
        @pl.when(z > 0)
        def _():
            act(piece(owner, k, 1, me - columns))

    start = lambda copy: copy.start()
    sent = lambda copy: copy.wait_send()
    landed = lambda copy: copy.wait_recv()

    for k in range(chunks):
        upward(me, k, start)
        downward(me, k, start)
        across(me, k, start)

    def relay(hop, carry):
        for k in range(chunks):
            @pl.when(z - hop >= 0)
            def _():
                owner = me - hop * columns
                landed(piece(owner, k, 0, me))
                upward(owner, k, start)
                across(owner, k, start)

            @pl.when(z + hop < levels)
            def _():
                owner = me + hop * columns
                landed(piece(owner, k, 1, me))
                downward(owner, k, start)
                across(owner, k, start)
        return carry

    lax.fori_loop(1, levels, relay, 0)

    def collect(level, carry):
        for j in range(1, columns):
            for k in range(chunks):
                landed(piece(level * columns + lax.rem(x + j, columns), k, 1 + j, me))
        return carry

    lax.fori_loop(0, levels, collect, 0)
    loads[2].wait()
    loads[3].wait()

    def trade(g):
        return pltpu.make_async_remote_copy(
            src_ref=outgoing.at[g], dst_ref=incoming.at[g],
            send_sem=pair_send.at[g], recv_sem=pair_recv.at[g],
            device_id={"query": 1 - core}, device_id_type=MESH,
        )

    def product(which, g):
        rows = gathered[which, pl.ds(g * per_group, per_group)].reshape(LANES, width)
        return lax.dot_general(
            train_v[...], rows, (((1,), (1,)), ((), ())), preferred_element_type=jnp.float32
        )

    def first(g, carry):
        outgoing[g] = product(1 - core, g)
        trade(g).start()
        return carry

    lax.fori_loop(0, groups, first, 0)

    def slot(owner):
        return owner // per_group * per_group + per_group - 1 - lax.rem(owner, per_group)

    def tops_of(g, best):
        place = lax.broadcasted_iota(jnp.int32, (8, LANES), 1) // half
        for h in range(TOPM // per_group):
            packed = None
            for i in range(per_group):
                turned = pltpu.roll(best[h * per_group + i], (i + 1) * half % LANES, 1)
                turned = pltpu.roll(turned, 0, 1, stride=half, stride_axis=0)
                packed = turned if packed is None else jnp.where(place == i, turned, packed)
            tops[pl.ds(g * per_group, per_group), h, :] = packed

    def best_of(g, carry):
        scores[...] = product(core, g)
        trade(g).wait()
        lane_owner = g * per_group + lax.broadcasted_iota(jnp.int32, (8, LANES), 1) // half

        def visit(b, best):
            named = lane_owner == pairs_ref[b, 0]
            for f in range(1, pairs_ref.shape[1]):
                named = named | (lane_owner == pairs_ref[b, f])
            vals = []
            for i in range(TBLK // 8):
                at = pl.ds(pl.multiple_of(b * TBLK + i * 8, 8), 8)
                total = scores[at, :] + incoming[g, at, :]
                vals.append(jnp.where(named, total, empty_fill))
            return tuple(merge_top(list(best), sort_falling(vals)))

        none = tuple(jnp.full((8, LANES), empty_fill, jnp.float32) for _ in range(TOPM))
        best = merge_sublanes(list(lax.fori_loop(0, train_blocks, visit, none)))
        tops_of(g, best)
        return carry

    lax.fori_loop(0, groups, best_of, 0)

    def deliver(step):
        peer = lax.rem(me + step, owners)
        return pltpu.make_async_remote_copy(
            src_ref=tops.at[slot(peer)], dst_ref=arrived.at[me],
            send_sem=top_send.at[peer], recv_sem=top_recv.at[me],
            device_id={"train": peer}, device_id_type=MESH,
        )

    def receive(step):
        peer = lax.rem(me + step, owners)
        return pltpu.make_async_remote_copy(
            src_ref=tops.at[0], dst_ref=arrived.at[peer],
            send_sem=top_send.at[peer], recv_sem=top_recv.at[peer],
            device_id={"train": peer}, device_id_type=MESH,
        )

    def each(act):
        def body(step, carry):
            act(step)
            return carry
        lax.fori_loop(1, owners, body, 0)

    each(lambda step: deliver(step).start())
    arrived[me] = tops[slot(me)]
    for k in range(chunks):
        upward(me, k, sent)
        downward(me, k, sent)
        across(me, k, sent)

    def drain(hop, carry):
        for k in range(chunks):
            @pl.when(z - hop >= 0)
            def _():
                upward(me - hop * columns, k, sent)
                across(me - hop * columns, k, sent)

            @pl.when(z + hop < levels)
            def _():
                downward(me + hop * columns, k, sent)
                across(me + hop * columns, k, sent)
        return carry

    lax.fori_loop(1, levels, drain, 0)
    each(lambda step: receive(step).wait_recv())

    best = None
    for s in range(owners // 8):
        lists = []
        for r in range(TOPM):
            row = arrived[s * 8:(s + 1) * 8, r // per_group, :]
            lists.append(pltpu.roll(row, (LANES - r % per_group * half) % LANES, 1))
        best = lists if best is None else merge_top(best, lists)
    best = merge_sublanes(best)
    ranked = jnp.concatenate([v[:1] for v in best], axis=0) * (1.0 / math.sqrt(K))
    square = jnp.concatenate(
        [ranked, jnp.zeros((LANES - TOPM, LANES), jnp.float32)], axis=0
    )
    out_ref[...] = square.T[:half, :TOPM]
    each(lambda step: deliver(step).wait_send())


def per_device(train_grads, query_grads, precond, pairs):
    owners = lax.axis_size("train")
    columns = 1
    for c in range(2, owners):
        if owners % c == 0 and c ** 3 <= owners:
            columns = c
    queries, width = query_grads.shape
    rows = train_grads.shape[0]
    chunks = 4 if owners <= 8 else 1
    half = queries // 2
    groups = owners * half // LANES
    f32 = jnp.float32
    return pl.pallas_call(
        functools.partial(kernel, owners, columns, chunks),
        out_shape=jax.ShapeDtypeStruct((half, TOPM), f32),
        in_specs=[pl.BlockSpec(memory_space=pl.ANY)] * 4,
        out_specs=pl.BlockSpec(memory_space=pltpu.VMEM),
        scratch_shapes=[
            pltpu.SMEM(pairs.shape, pairs.dtype),
            pltpu.VMEM(query_grads.shape, query_grads.dtype),
            pltpu.VMEM(precond.shape, precond.dtype),
            pltpu.VMEM(train_grads.shape, train_grads.dtype),
            pltpu.VMEM((2, owners, half, width), jnp.bfloat16),
            pltpu.VMEM((groups, rows, LANES), f32),
            pltpu.VMEM((groups, rows, LANES), f32),
            pltpu.VMEM((rows, LANES), f32),
            pltpu.VMEM((owners, TOPM * half // LANES, LANES), f32),
            pltpu.VMEM((owners, TOPM * half // LANES, LANES), f32),
            pltpu.SemaphoreType.DMA((4,)),
            pltpu.SemaphoreType.DMA((1 + columns, owners, chunks)),
            pltpu.SemaphoreType.DMA((owners, chunks)),
            pltpu.SemaphoreType.DMA((groups,)),
            pltpu.SemaphoreType.DMA((groups,)),
            pltpu.SemaphoreType.DMA((owners,)),
            pltpu.SemaphoreType.DMA((owners,)),
        ],
        compiler_params=pltpu.CompilerParams(
            collective_id=0, has_side_effects=True, vmem_limit_bytes=63 * 1024 * 1024
        ),
    )(query_grads, precond, train_grads, pairs)


def solution(mesh):
    placed = (
        P(("groups", "train"), "query"),
        P(("groups", "train"), "query"),
        P("query", None, None),
        P(("groups", "train"), None),
    )
    return jax.shard_map(
        per_device,
        mesh=mesh,
        in_specs=placed,
        out_specs=P(("groups", "train", "query"), None),
        check_vma=False,
    )
```

```python
import functools
import math

import jax
import jax.numpy as jnp
from jax import lax
from jax.experimental import pallas as pl
from jax.experimental.pallas import tpu as pltpu
from jax.sharding import PartitionSpec as P

K = 4096
TBLK = 128
TOPM = 16
LANES = 128
MESH = pl.DeviceIdType.MESH

empty_fill = -1e30


def exchange(xs, i, j):
    a, b = xs[i], xs[j]
    xs[i], xs[j] = jnp.maximum(a, b), jnp.minimum(a, b)


def sort_falling(xs):
    xs = list(xs)
    n = len(xs)
    p = 1
    while p < n:
        k = p
        while k >= 1:
            for j in range(k % p, n - k, 2 * k):
                for i in range(min(k, n - j - k)):
                    if (i + j) // (2 * p) == (i + j + k) // (2 * p):
                        exchange(xs, i + j, i + j + k)
            k //= 2
        p *= 2
    return xs


def merge_top(xs, ys):
    n = len(xs)
    out = [jnp.maximum(xs[i], ys[n - 1 - i]) for i in range(n)]
    step = n // 2
    while step >= 1:
        for i in range(n):
            if i & step == 0:
                exchange(out, i, i + step)
        step //= 2
    return out


def merge_sublanes(xs):
    for shift in (4, 2, 1):
        xs = merge_top(xs, [pltpu.roll(x, shift, 0) for x in xs])
    return xs


def kernel(
    owners, columns, chunks,
    query_hbm, precond_hbm, train_hbm, pairs_hbm, out_ref,
    pairs_ref, query_v, precond_v, train_v, gathered, outgoing, incoming, scores, tops, arrived,
    load_sem, send_sem, recv_sem, pair_send, pair_recv, top_send, top_recv,
):
    me = lax.axis_index("train")
    core = lax.axis_index("query")
    x, z = lax.rem(me, columns), me // columns
    levels = owners // columns
    width = query_v.shape[1]
    chunk = width // chunks
    size = precond_v.shape[1]
    half = query_v.shape[0] // 2
    train_blocks = train_v.shape[0] // TBLK
    groups = owners * half // LANES
    per_group = LANES // half

    loads = [
        pltpu.make_async_copy(query_hbm, query_v, load_sem.at[0]),
        pltpu.make_async_copy(precond_hbm, precond_v, load_sem.at[1]),
        pltpu.make_async_copy(train_hbm, train_v, load_sem.at[2]),
        pltpu.make_async_copy(pairs_hbm, pairs_ref, load_sem.at[3]),
    ]
    for load in loads:
        load.start()

    barrier = pltpu.get_barrier_semaphore()

    def greet(peer):
        pl.semaphore_signal(barrier, inc=1, device_id={"train": peer}, device_id_type=MESH)

    pl.when(z > 0)(lambda: greet(me - columns))
    pl.when(z < levels - 1)(lambda: greet(me + columns))
    for j in range(1, columns):
        greet(z * columns + lax.rem(x + j, columns))
    pl.semaphore_signal(barrier, inc=1, device_id={"query": 1 - core}, device_id_type=MESH)

    loads[0].wait()
    loads[1].wait()
    for j in range(precond_v.shape[0]):
        part = jnp.dot(
            query_v[:, j * size:(j + 1) * size], precond_v[j], preferred_element_type=jnp.float32
        ).astype(jnp.bfloat16)
        gathered[0, me, :, j * size:(j + 1) * size] = part[:half]
        gathered[1, me, :, j * size:(j + 1) * size] = part[half:]
    lower, upper = (z + levels - 1) // levels, (2 * levels - 2 - z) // levels
    pl.semaphore_wait(barrier, columns + lower + upper)

    def piece(owner, k, way, peer):
        ref = gathered.at[:, owner, :, pl.ds(k * chunk, chunk)]
        return pltpu.make_async_remote_copy(
            src_ref=ref, dst_ref=ref,
            send_sem=send_sem.at[way, owner, k], recv_sem=recv_sem.at[owner, k],
            device_id={"train": peer}, device_id_type=MESH,
        )

    def across(owner, k, act):
        for j in range(1, columns):
            act(piece(owner, k, 1 + j, z * columns + lax.rem(x + j, columns)))

    def upward(owner, k, act):
        @pl.when(z < levels - 1)
        def _():
            act(piece(owner, k, 0, me + columns))

    def downward(owner, k, act):
        @pl.when(z > 0)
        def _():
            act(piece(owner, k, 1, me - columns))

    def below(hop, k, before, act):
        @pl.when(z - hop >= 0)
        def _():
            owner = me - hop * columns
            before(owner)
            upward(owner, k, act)
            across(owner, k, act)

    def above(hop, k, before, act):
        @pl.when(z + hop < levels)
        def _():
            owner = me + hop * columns
            before(owner)
            downward(owner, k, act)
            across(owner, k, act)

    start = lambda copy: copy.start()
    sent = lambda copy: copy.wait_send()
    landed = lambda copy: copy.wait_recv()

    def collect(k):
        for j in range(1, columns):
            for step in range(levels):
                owner = lax.rem(z + step, levels) * columns + lax.rem(x + j, columns)
                landed(piece(owner, k, 1 + j, me))

    def trade(g):
        return pltpu.make_async_remote_copy(
            src_ref=outgoing.at[g], dst_ref=incoming.at[g],
            send_sem=pair_send.at[g], recv_sem=pair_recv.at[g],
            device_id={"query": 1 - core}, device_id_type=MESH,
        )

    def product(which, g, k):
        part = slice(k * chunk, (k + 1) * chunk)
        rows = gathered[which, pl.ds(g * per_group, per_group), :, part].reshape(LANES, chunk)
        return lax.dot_general(
            train_v[:, part], rows, (((1,), (1,)), ((), ())), preferred_element_type=jnp.float32
        )

    def multiply(k):
        collect(k)
        if k == 0:
            loads[2].wait()

        def other(g, carry):
            found = product(1 - core, g, k)
            outgoing[g] = found if k == 0 else outgoing[g] + found
            if k == chunks - 1:
                trade(g).start()
            return carry

        def own(g, carry):
            found = product(core, g, k)
            scores[g] = found if k == 0 else scores[g] + found
            return carry

        lax.fori_loop(0, groups, other, 0)
        lax.fori_loop(0, groups, own, 0)

    for wave in range(levels + chunks - 1):
        if wave < chunks:
            upward(me, wave, start)
            downward(me, wave, start)
            across(me, wave, start)
        for hop in range(1, levels):
            k = wave - hop
            if 0 <= k < chunks:
                below(hop, k, lambda owner: landed(piece(owner, k, 0, me)), start)
                above(hop, k, lambda owner: landed(piece(owner, k, 1, me)), start)
        if 0 <= wave - levels < chunks:
            multiply(wave - levels)
    multiply(chunks - 1)
    loads[3].wait()

    def slot(owner):
        return owner // per_group * per_group + per_group - 1 - lax.rem(owner, per_group)

    def tops_of(g, best):
        place = lax.broadcasted_iota(jnp.int32, (8, LANES), 1) // half
        for h in range(TOPM // per_group):
            packed = None
            for i in range(per_group):
                turned = pltpu.roll(best[h * per_group + i], (i + 1) * half % LANES, 1)
                turned = pltpu.roll(turned, 0, 1, stride=half, stride_axis=0)
                packed = turned if packed is None else jnp.where(place == i, turned, packed)
            tops[pl.ds(g * per_group, per_group), h, :] = packed

    def best_of(g, carry):
        trade(g).wait()
        lane_owner = g * per_group + lax.broadcasted_iota(jnp.int32, (8, LANES), 1) // half

        def visit(b, best):
            named = lane_owner == pairs_ref[b, 0]
            for f in range(1, pairs_ref.shape[1]):
                named = named | (lane_owner == pairs_ref[b, f])
            vals = []
            for i in range(TBLK // 8):
                at = pl.ds(pl.multiple_of(b * TBLK + i * 8, 8), 8)
                total = scores[g, at, :] + incoming[g, at, :]
                vals.append(jnp.where(named, total, empty_fill))
            return tuple(merge_top(list(best), sort_falling(vals)))

        none = tuple(jnp.full((8, LANES), empty_fill, jnp.float32) for _ in range(TOPM))
        best = merge_sublanes(list(lax.fori_loop(0, train_blocks, visit, none)))
        tops_of(g, best)
        return carry

    lax.fori_loop(0, groups, best_of, 0)

    def deliver(step):
        peer = lax.rem(me + step, owners)
        return pltpu.make_async_remote_copy(
            src_ref=tops.at[slot(peer)], dst_ref=arrived.at[me],
            send_sem=top_send.at[peer], recv_sem=top_recv.at[me],
            device_id={"train": peer}, device_id_type=MESH,
        )

    def receive(step):
        peer = lax.rem(me + step, owners)
        return pltpu.make_async_remote_copy(
            src_ref=tops.at[0], dst_ref=arrived.at[peer],
            send_sem=top_send.at[peer], recv_sem=top_recv.at[peer],
            device_id={"train": peer}, device_id_type=MESH,
        )

    def each(act):
        def body(step, carry):
            act(step)
            return carry
        lax.fori_loop(1, owners, body, 0)

    each(lambda step: deliver(step).start())
    arrived[me] = tops[slot(me)]
    for k in range(chunks):
        upward(me, k, sent)
        downward(me, k, sent)
        across(me, k, sent)
        for hop in range(1, levels):
            below(hop, k, lambda owner: None, sent)
            above(hop, k, lambda owner: None, sent)

    each(lambda step: receive(step).wait_recv())

    best = None
    for s in range(owners // 8):
        lists = []
        for r in range(TOPM):
            row = arrived[s * 8:(s + 1) * 8, r // per_group, :]
            lists.append(pltpu.roll(row, (LANES - r % per_group * half) % LANES, 1))
        best = lists if best is None else merge_top(best, lists)
    best = merge_sublanes(best)
    ranked = jnp.concatenate([v[:1] for v in best], axis=0) * (1.0 / math.sqrt(K))
    square = jnp.concatenate(
        [ranked, jnp.zeros((LANES - TOPM, LANES), jnp.float32)], axis=0
    )
    out_ref[...] = square.T[:half, :TOPM]
    each(lambda step: deliver(step).wait_send())


def per_device(train_grads, query_grads, precond, pairs):
    owners = lax.axis_size("train")
    columns = 1
    for c in range(2, owners):
        if owners % c == 0 and c ** 3 <= owners:
            columns = c
    queries, width = query_grads.shape
    rows = train_grads.shape[0]
    chunks = 2 if owners <= 8 else 1
    half = queries // 2
    groups = owners * half // LANES
    f32 = jnp.float32
    return pl.pallas_call(
        functools.partial(kernel, owners, columns, chunks),
        out_shape=jax.ShapeDtypeStruct((half, TOPM), f32),
        in_specs=[pl.BlockSpec(memory_space=pl.ANY)] * 4,
        out_specs=pl.BlockSpec(memory_space=pltpu.VMEM),
        scratch_shapes=[
            pltpu.SMEM(pairs.shape, pairs.dtype),
            pltpu.VMEM(query_grads.shape, query_grads.dtype),
            pltpu.VMEM(precond.shape, precond.dtype),
            pltpu.VMEM(train_grads.shape, train_grads.dtype),
            pltpu.VMEM((2, owners, half, width), jnp.bfloat16),
            pltpu.VMEM((groups, rows, LANES), f32),
            pltpu.VMEM((groups, rows, LANES), f32),
            pltpu.VMEM((groups, rows, LANES), f32),
            pltpu.VMEM((owners, TOPM * half // LANES, LANES), f32),
            pltpu.VMEM((owners, TOPM * half // LANES, LANES), f32),
            pltpu.SemaphoreType.DMA((4,)),
            pltpu.SemaphoreType.DMA((1 + columns, owners, chunks)),
            pltpu.SemaphoreType.DMA((owners, chunks)),
            pltpu.SemaphoreType.DMA((groups,)),
            pltpu.SemaphoreType.DMA((groups,)),
            pltpu.SemaphoreType.DMA((owners,)),
            pltpu.SemaphoreType.DMA((owners,)),
        ],
        compiler_params=pltpu.CompilerParams(
            collective_id=0, has_side_effects=True, vmem_limit_bytes=63 * 1024 * 1024
        ),
    )(query_grads, precond, train_grads, pairs)


def solution(mesh):
    placed = (
        P(("groups", "train"), "query"),
        P(("groups", "train"), "query"),
        P("query", None, None),
        P(("groups", "train"), None),
    )
    return jax.shard_map(
        per_device,
        mesh=mesh,
        in_specs=placed,
        out_specs=P(("groups", "train", "query"), None),
        check_vma=False,
    )
```

```python
import functools
import math

import jax
import jax.numpy as jnp
from jax import lax
from jax.experimental import pallas as pl
from jax.experimental.pallas import tpu as pltpu
from jax.sharding import PartitionSpec as P

K = 4096
TBLK = 128
TOPM = 16
LANES = 128
MESH = pl.DeviceIdType.MESH

empty_fill = -1e30


def exchange(xs, i, j):
    a, b = xs[i], xs[j]
    xs[i], xs[j] = jnp.maximum(a, b), jnp.minimum(a, b)


def sort_falling(xs):
    xs = list(xs)
    n = len(xs)
    p = 1
    while p < n:
        k = p
        while k >= 1:
            for j in range(k % p, n - k, 2 * k):
                for i in range(min(k, n - j - k)):
                    if (i + j) // (2 * p) == (i + j + k) // (2 * p):
                        exchange(xs, i + j, i + j + k)
            k //= 2
        p *= 2
    return xs


def merge_top(xs, ys):
    n = len(xs)
    out = [jnp.maximum(xs[i], ys[n - 1 - i]) for i in range(n)]
    step = n // 2
    while step >= 1:
        for i in range(n):
            if i & step == 0:
                exchange(out, i, i + step)
        step //= 2
    return out


def merge_sublanes(xs):
    for shift in (4, 2, 1):
        xs = merge_top(xs, [pltpu.roll(x, shift, 0) for x in xs])
    return xs


def kernel(
    owners, columns, chunks,
    query_hbm, precond_hbm, train_hbm, pairs_hbm, out_ref,
    pairs_ref, query_v, precond_v, train_v, gathered, outgoing, incoming, scores, tops, arrived,
    load_sem, send_sem, recv_sem, pair_send, pair_recv, top_send, top_recv,
):
    me = lax.axis_index("train")
    core = lax.axis_index("query")
    x, z = lax.rem(me, columns), me // columns
    levels = owners // columns
    width = query_v.shape[1]
    chunk = width // chunks
    size = precond_v.shape[1]
    half = query_v.shape[0] // 2
    train_blocks = train_v.shape[0] // TBLK
    groups = owners * half // LANES
    per_group = LANES // half

    loads = [
        pltpu.make_async_copy(query_hbm, query_v, load_sem.at[0]),
        pltpu.make_async_copy(precond_hbm, precond_v, load_sem.at[1]),
        pltpu.make_async_copy(train_hbm, train_v, load_sem.at[2]),
        pltpu.make_async_copy(pairs_hbm, pairs_ref, load_sem.at[3]),
    ]
    for load in loads:
        load.start()

    barrier = pltpu.get_barrier_semaphore()

    def greet(peer):
        pl.semaphore_signal(barrier, inc=1, device_id={"train": peer}, device_id_type=MESH)

    pl.when(z > 0)(lambda: greet(me - columns))
    pl.when(z < levels - 1)(lambda: greet(me + columns))
    for j in range(1, columns):
        greet(z * columns + lax.rem(x + j, columns))
    pl.semaphore_signal(barrier, inc=1, device_id={"query": 1 - core}, device_id_type=MESH)

    loads[0].wait()
    loads[1].wait()
    for j in range(precond_v.shape[0]):
        part = jnp.dot(
            query_v[:, j * size:(j + 1) * size], precond_v[j], preferred_element_type=jnp.float32
        ).astype(jnp.bfloat16)
        gathered[0, me, :, j * size:(j + 1) * size] = part[:half]
        gathered[1, me, :, j * size:(j + 1) * size] = part[half:]
    lower, upper = (z + levels - 1) // levels, (2 * levels - 2 - z) // levels
    pl.semaphore_wait(barrier, columns + lower + upper)

    def piece(owner, k, way, peer):
        ref = gathered.at[:, owner, :, pl.ds(k * chunk, chunk)]
        return pltpu.make_async_remote_copy(
            src_ref=ref, dst_ref=ref,
            send_sem=send_sem.at[way, owner, k], recv_sem=recv_sem.at[owner, k],
            device_id={"train": peer}, device_id_type=MESH,
        )

    def across(owner, k, act):
        for j in range(1, columns):
            act(piece(owner, k, 1 + j, z * columns + lax.rem(x + j, columns)))

    def upward(owner, k, act):
        @pl.when(z < levels - 1)
        def _():
            act(piece(owner, k, 0, me + columns))

    def downward(owner, k, act):
        @pl.when(z > 0)
        def _():
            act(piece(owner, k, 1, me - columns))

    def below(hop, k, before, act):
        @pl.when(z - hop >= 0)
        def _():
            owner = me - hop * columns
            before(owner)
            upward(owner, k, act)
            across(owner, k, act)

    def above(hop, k, before, act):
        @pl.when(z + hop < levels)
        def _():
            owner = me + hop * columns
            before(owner)
            downward(owner, k, act)
            across(owner, k, act)

    start = lambda copy: copy.start()
    sent = lambda copy: copy.wait_send()
    landed = lambda copy: copy.wait_recv()

    def collect(k):
        for j in range(1, columns):
            for step in range(levels):
                owner = lax.rem(z + step, levels) * columns + lax.rem(x + j, columns)
                landed(piece(owner, k, 1 + j, me))

    def trade(g):
        return pltpu.make_async_remote_copy(
            src_ref=outgoing.at[g], dst_ref=incoming.at[g],
            send_sem=pair_send.at[g], recv_sem=pair_recv.at[g],
            device_id={"query": 1 - core}, device_id_type=MESH,
        )

    def product(which, g, k):
        part = slice(k * chunk, (k + 1) * chunk)
        rows = gathered[which, pl.ds(g * per_group, per_group), :, part].reshape(LANES, chunk)
        return lax.dot_general(
            train_v[:, part], rows, (((1,), (1,)), ((), ())), preferred_element_type=jnp.float32
        )

    def multiply(k):
        collect(k)
        if k == 0:
            loads[2].wait()

        def other(g, carry):
            found = product(1 - core, g, k)
            outgoing[g] = found if k == 0 else outgoing[g] + found
            if k == chunks - 1:
                trade(g).start()
            return carry

        def own(g, carry):
            found = product(core, g, k)
            scores[g] = found if k == 0 else scores[g] + found
            return carry

        lax.fori_loop(0, groups, other, 0)
        lax.fori_loop(0, groups, own, 0)

    for k in range(chunks):
        upward(me, k, start)
        downward(me, k, start)
        across(me, k, start)
    for hop in range(1, levels):
        for k in range(chunks):
            below(hop, k, lambda owner: landed(piece(owner, k, 0, me)), start)
            above(hop, k, lambda owner: landed(piece(owner, k, 1, me)), start)
    for k in range(chunks - 1):
        multiply(k)
    for k in range(chunks):
        upward(me, k, sent)
        downward(me, k, sent)
        across(me, k, sent)
        for hop in range(1, levels):
            below(hop, k, lambda owner: None, sent)
            above(hop, k, lambda owner: None, sent)

    multiply(chunks - 1)
    loads[3].wait()

    def slot(owner):
        return owner // per_group * per_group + per_group - 1 - lax.rem(owner, per_group)

    def tops_of(g, best):
        place = lax.broadcasted_iota(jnp.int32, (8, LANES), 1) // half
        for h in range(TOPM // per_group):
            packed = None
            for i in range(per_group):
                turned = pltpu.roll(best[h * per_group + i], (i + 1) * half % LANES, 1)
                turned = pltpu.roll(turned, 0, 1, stride=half, stride_axis=0)
                packed = turned if packed is None else jnp.where(place == i, turned, packed)
            tops[pl.ds(g * per_group, per_group), h, :] = packed

    def best_of(g, carry):
        trade(g).wait()
        lane_owner = g * per_group + lax.broadcasted_iota(jnp.int32, (8, LANES), 1) // half

        def visit(b, best):
            named = lane_owner == pairs_ref[b, 0]
            for f in range(1, pairs_ref.shape[1]):
                named = named | (lane_owner == pairs_ref[b, f])
            vals = []
            for i in range(TBLK // 8):
                at = pl.ds(pl.multiple_of(b * TBLK + i * 8, 8), 8)
                total = scores[g, at, :] + incoming[g, at, :]
                vals.append(jnp.where(named, total, empty_fill))
            return tuple(merge_top(list(best), sort_falling(vals)))

        none = tuple(jnp.full((8, LANES), empty_fill, jnp.float32) for _ in range(TOPM))
        best = merge_sublanes(list(lax.fori_loop(0, train_blocks, visit, none)))
        tops_of(g, best)
        return carry

    lax.fori_loop(0, groups, best_of, 0)

    def deliver(step):
        peer = lax.rem(me + step, owners)
        return pltpu.make_async_remote_copy(
            src_ref=tops.at[slot(peer)], dst_ref=arrived.at[me],
            send_sem=top_send.at[peer], recv_sem=top_recv.at[me],
            device_id={"train": peer}, device_id_type=MESH,
        )

    def receive(step):
        peer = lax.rem(me + step, owners)
        return pltpu.make_async_remote_copy(
            src_ref=tops.at[0], dst_ref=arrived.at[peer],
            send_sem=top_send.at[peer], recv_sem=top_recv.at[peer],
            device_id={"train": peer}, device_id_type=MESH,
        )

    def each(act):
        def body(step, carry):
            act(step)
            return carry
        lax.fori_loop(1, owners, body, 0)

    each(lambda step: deliver(step).start())
    arrived[me] = tops[slot(me)]
    each(lambda step: receive(step).wait_recv())

    best = None
    for s in range(owners // 8):
        lists = []
        for r in range(TOPM):
            row = arrived[s * 8:(s + 1) * 8, r // per_group, :]
            lists.append(pltpu.roll(row, (LANES - r % per_group * half) % LANES, 1))
        best = lists if best is None else merge_top(best, lists)
    best = merge_sublanes(best)
    ranked = jnp.concatenate([v[:1] for v in best], axis=0) * (1.0 / math.sqrt(K))
    square = jnp.concatenate(
        [ranked, jnp.zeros((LANES - TOPM, LANES), jnp.float32)], axis=0
    )
    out_ref[...] = square.T[:half, :TOPM]
    each(lambda step: deliver(step).wait_send())


def per_device(train_grads, query_grads, precond, pairs):
    owners = lax.axis_size("train")
    columns = 1
    for c in range(2, owners):
        if owners % c == 0 and c ** 3 <= owners:
            columns = c
    queries, width = query_grads.shape
    rows = train_grads.shape[0]
    chunks = 2 if owners <= 8 else 1
    half = queries // 2
    groups = owners * half // LANES
    f32 = jnp.float32
    return pl.pallas_call(
        functools.partial(kernel, owners, columns, chunks),
        out_shape=jax.ShapeDtypeStruct((half, TOPM), f32),
        in_specs=[pl.BlockSpec(memory_space=pl.ANY)] * 4,
        out_specs=pl.BlockSpec(memory_space=pltpu.VMEM),
        scratch_shapes=[
            pltpu.SMEM(pairs.shape, pairs.dtype),
            pltpu.VMEM(query_grads.shape, query_grads.dtype),
            pltpu.VMEM(precond.shape, precond.dtype),
            pltpu.VMEM(train_grads.shape, train_grads.dtype),
            pltpu.VMEM((2, owners, half, width), jnp.bfloat16),
            pltpu.VMEM((groups, rows, LANES), f32),
            pltpu.VMEM((groups, rows, LANES), f32),
            pltpu.VMEM((groups, rows, LANES), f32),
            pltpu.VMEM((owners, TOPM * half // LANES, LANES), f32),
            pltpu.VMEM((owners, TOPM * half // LANES, LANES), f32),
            pltpu.SemaphoreType.DMA((4,)),
            pltpu.SemaphoreType.DMA((1 + columns, owners, chunks)),
            pltpu.SemaphoreType.DMA((owners, chunks)),
            pltpu.SemaphoreType.DMA((groups,)),
            pltpu.SemaphoreType.DMA((groups,)),
            pltpu.SemaphoreType.DMA((owners,)),
            pltpu.SemaphoreType.DMA((owners,)),
        ],
        compiler_params=pltpu.CompilerParams(
            collective_id=0, has_side_effects=True, vmem_limit_bytes=63 * 1024 * 1024
        ),
    )(query_grads, precond, train_grads, pairs)


def solution(mesh):
    placed = (
        P(("groups", "train"), "query"),
        P(("groups", "train"), "query"),
        P("query", None, None),
        P(("groups", "train"), None),
    )
    return jax.shard_map(
        per_device,
        mesh=mesh,
        in_specs=placed,
        out_specs=P(("groups", "train", "query"), None),
        check_vma=False,
    )
```
